32 devices in a mesh: px: 4 (over z), py: 8 (over y, x, core).
Axes of the slice: x: 2, y: 2, z: 4, core: 2. Of those that a mesh axis runs over, the one named last changes fastest.
Arguments:
- background_field: float32 [32, 256, 1024], P('px', 'py'), may hold values from -6 to 6
- perturbation: float32 [32, 256, 1024], P('px', 'py'), may hold values from -6 to 6
- permittivity: float32 [32, 256, 1024], P('px', 'py'), may hold values from 0.5 to 2
- probe_nodes: int32 [4, 32768], P(None, ('px', 'py')), may hold values from 0 to 262143
- probe_weights: float32 [4, 32768], P(None, ('px', 'py')), may hold values from 0.1 to 1
- probe_owner: int32 [32768, 1], P(('px', 'py')), may hold values from 0 to 31; in each aligned block of 1024 rows (0 to 1023, 1024 to 2047, ...) at most 64 rows name the same one
- probe_sensor: int32 [32768], P(('px', 'py')), may hold values from 0 to 7
- sensor_weight: float32 [256], P(('px', 'py')), may hold values from 0.2 to 5
Outputs:
- hess_vec: float32 [32, 256, 1024], P('px', 'py')
The draws below stay inside these ranges and needn't reach their ends.
Inputs may be any that keep to these rules, and one draw needn't show every extreme that they name: `probe_nodes`: each probe's nodes lie in the block of the device that holds the probe. `probe_owner`: of the probes of one device at most 64 name the same owner, and in every draw some owner is named by exactly 64 of them.
All inputs are finite; a program needn't handle non-finite values.
Results may differ from the reference program's by a relative error of at most 0.00025.
Values sent between devices are 32-bit elements; how exact they have to be, the bound alone decides.
A program may use at most 64 MiB of HBM per device.

```python
import math
import jax
import jax.numpy as jnp
import numpy as np
from jax import lax

CX = 8
CY = 32
CZ = 1024
PROBE_DEV = 1024
SENS_DEV = 8
SWEEPS = 4
CAP = 64
NX = 32
NY = 256
NZ = 1024
PROBES = 32768
SENSORS = 256
N_PX = 4
N_PY = 8


def with_ends(values, rng, low, largest):
    longest = values.shape.index(max(values.shape))
    spots = []
    for shift in (0, 1):
        where = [jax.random.randint(jax.random.fold_in(rng, axis), (), 0, length) for axis, length in enumerate(values.shape)]
        where[longest] = (where[longest] + shift) % values.shape[longest]
        spots.append(tuple(where))
    return values.at[spots[0]].set(low).at[spots[1]].set(largest)


def block_levels(key, dims, split, low, top_value):
    level = 1.0
    for dim, shards_of in split:
        steps = jax.random.uniform(jax.random.fold_in(jax.random.fold_in(key, 6), dim), (shards_of,), jnp.float32, low / len(split), top_value / len(split))
        level = level * jnp.repeat(jnp.exp(steps), dims[dim] // shards_of).reshape((-1,) + (1,) * (len(dims) - 1 - dim))
    return level


def assign_block(rng, own, number, rows, count, top, reach, lean):
    sequence = jax.random.permutation(rng, count)
    packed, ordinary = load_shares(count, rows * top, reach, lean, True), load_shares(count, rows * top, reach, lean, False)
    places = jnp.arange(count)

    def named(lengths, turn):
        used = int((lengths > 0).sum())
        fixed = max(1, used // 4)
        shifted = fixed + (places - fixed + turn * (used - fixed)) % max(1, count - fixed)
        return jnp.zeros((count,), jnp.int32).at[sequence[jnp.where(places < fixed, places, shifted)]].set(jnp.asarray(lengths, jnp.int32))

    lengths = jnp.where(number % 4 == 0, named(packed, number // 4), named(ordinary, number - number // 4 - 1))
    mixed = jax.random.permutation(jax.random.fold_in(own, 3), count)
    source_of, taker = mixed[0:count // 2 * 2:2], mixed[1:count // 2 * 2:2]
    slack = jnp.minimum(lengths[source_of] - 1, reach - lengths[taker]) // 2
    slack = jnp.where((source_of == sequence[0]) | (taker == sequence[0]) | (lengths[taker] == 0), 0, jnp.maximum(slack, 0))
    shifted = jax.random.randint(jax.random.fold_in(own, 4), (count // 2,), 0, 1 << 20) % (slack + 1)
    lengths = lengths.at[source_of].add(-shifted).at[taker].add(shifted)
    items = jnp.searchsorted(jnp.cumsum(lengths), jnp.arange(rows * top), side="right").astype(jnp.int32)
    grid = items.reshape(top, rows).T
    grid = grid[jax.random.permutation(jax.random.fold_in(own, 1), rows)]
    turn = jax.random.randint(jax.random.fold_in(own, 2), (rows, 1), 0, top)
    return jnp.take_along_axis(grid, (jnp.arange(top)[None, :] + turn) % top, axis=1)


def load_shares(amount, total, most, skew, full):
    weights = [(1 << 20) // math.isqrt(rank ** skew) + 1 for rank in range(1, amount + 1)]
    largest = most if full else min(most, max(-(-total // amount), total * weights[0] // sum(weights)))
    least = 1 if total - largest >= amount - 1 else 0
    given, surplus = [largest] + [least] * (amount - 1), total - largest - least * (amount - 1)
    while surplus > 0:
        free = [i for i in range(1, amount) if given[i] < largest] or [i for i in range(1, amount) if given[i] < most]
        pool, remaining = sum([weights[i] for i in free]), surplus
        for i in free:
            extra = min(most - given[i], max(1, remaining * weights[i] // pool), surplus)
            given[i] = given[i] + extra
            surplus = surplus - extra
    return np.array(given)


def gaussian(stream_key, shape, width, bound, shards=(), kind=jnp.bfloat16):
    entries = jax.random.normal(stream_key, shape, jnp.float32) * width
    if len(shards) > 0:
        entries = block_levels(stream_key, shape, shards, -0.22, 0.18) * entries
    return jnp.clip(entries, min=-bound, max=bound).astype(kind)


def setup_inputs(seed: int = 0) -> dict:
    streams_of = jax.random.split(jax.random.key(seed), 9)
    background_field = gaussian(streams_of[0], (NX, NY, NZ), 1.0, 6.0, ((0, 4), (1, 8)), jnp.float32)
    perturbation = gaussian(streams_of[1], (NX, NY, NZ), 1.0, 6.0, ((0, 4), (1, 8)), jnp.float32)
    permittivity = jnp.clip(jnp.exp(math.log(2.0) - 1.3862944 * jax.random.uniform(streams_of[2], (NX, NY, NZ), jnp.float32) ** block_levels(streams_of[2], (NX, NY, NZ), ((0, 4), (1, 8)), -0.2, 0.2)), 0.5, 2.0)
    probe_nodes = with_ends(jax.random.randint(streams_of[3], (4, PROBES), 0, CX * CY * CZ), jax.random.fold_in(streams_of[3], 1), 0, (CX * CY * CZ) - 1).astype(jnp.int32)
    probe_weights = jnp.clip(0.1 + 0.9 * jax.random.uniform(streams_of[4], (4, PROBES), jnp.float32) ** block_levels(streams_of[4], (4, PROBES), ((1, 32),), -0.2, 0.2), 0.1, 1.0)
    probe_owner_keys = jax.random.split(jax.random.fold_in(streams_of[5], 1), PROBES // PROBE_DEV)
    probe_owner_turns = jax.random.permutation(jax.random.fold_in(streams_of[5], 3), PROBES // PROBE_DEV)
    probe_owner = jax.vmap(lambda own, number: assign_block(jax.random.fold_in(streams_of[5], 2), own, number, PROBE_DEV, N_PX * N_PY, 1, CAP, 2))(probe_owner_keys, probe_owner_turns).reshape((PROBES, 1))
    probe_sensor = with_ends(jax.random.randint(streams_of[6], (PROBES,), 0, SENS_DEV), jax.random.fold_in(streams_of[6], 1), 0, SENS_DEV - 1).astype(jnp.int32)
    sensor_weight = jnp.clip(jnp.exp(math.log(5.0) - 3.218876 * jax.random.uniform(streams_of[7], (SENSORS,), jnp.float32) ** block_levels(streams_of[7], (SENSORS,), ((0, 32),), -0.2, 0.2)), 0.2, 5.0)
    return dict(background_field=background_field, perturbation=perturbation, permittivity=permittivity, probe_nodes=probe_nodes, probe_weights=probe_weights, probe_owner=probe_owner, probe_sensor=probe_sensor, sensor_weight=sensor_weight)


mass_term = 1.0
bound_low = 1.0
bound_high = 25.0


def widen(array, direction, before, after):
    widths = [(0, 0), (0, 0), (0, 0)]
    widths[direction] = (before, after)
    return jnp.pad(array, widths)


def stiffness(field, permit, mass_value):
    result = mass_value * field
    for direction in range(3):
        extent = field.shape[direction]
        upper_cells = lax.slice_in_dim(field, 1, extent, axis=direction)
        lower_cells = lax.slice_in_dim(field, 0, extent - 1, axis=direction)
        face_coef = 0.5 * (lax.slice_in_dim(permit, 1, extent, axis=direction) + lax.slice_in_dim(permit, 0, extent - 1, axis=direction))
        face_flux = face_coef * (upper_cells - lower_cells)
        result = result - widen(face_flux, direction, 0, 1) + widen(face_flux, direction, 1, 0)
    return result


def chebyshev(source, permit):
    centre = 0.5 * (bound_high + bound_low)
    half_width = 0.5 * (bound_high - bound_low)
    spread = centre / half_width
    iterate = jnp.zeros_like(source)
    remain = source
    search = source / centre
    ratio_now = 1.0 / spread
    for sweep in range(SWEEPS):
        iterate = iterate + search
        if sweep < SWEEPS - 1:
            remain = remain - stiffness(search, permit, mass_term)
            ratio_next = 1.0 / (2.0 * spread - ratio_now)
            search = (ratio_next * ratio_now) * search + (2.0 * ratio_next / half_width) * remain
            ratio_now = ratio_next
    return iterate


def sensitivity(background, adjoint):
    total = jnp.zeros_like(background)
    for direction in range(3):
        extent = background.shape[direction]
        back_step = lax.slice_in_dim(background, 1, extent, axis=direction) - lax.slice_in_dim(background, 0, extent - 1, axis=direction)
        adj_step = lax.slice_in_dim(adjoint, 1, extent, axis=direction) - lax.slice_in_dim(adjoint, 0, extent - 1, axis=direction)
        product = back_step * adj_step
        total = total + widen(product, direction, 0, 1) + widen(product, direction, 1, 0)
    return -0.5 * total


def reference(background_field, perturbation, permittivity, probe_nodes, probe_weights, probe_owner, probe_sensor, sensor_weight):
    tangent = chebyshev(-stiffness(background_field, perturbation, 0.0), permittivity)
    total_x, total_y, total_z = tangent.shape
    probe_ids = jnp.arange(probe_sensor.shape[0], dtype=jnp.int32)
    device = probe_ids // PROBE_DEV
    block_x = device // N_PY
    block_y = device % N_PY
    local_x = probe_nodes // (CY * CZ)
    local_y = (probe_nodes // CZ) % CY
    local_z = probe_nodes % CZ
    global_x = block_x[None, :] * CX + local_x
    global_y = block_y[None, :] * CY + local_y
    global_nodes = ((global_x * total_y + global_y) * total_z + local_z).astype(jnp.int32)
    flat = tangent.reshape(-1)
    values = jnp.sum(probe_weights * flat[global_nodes], axis=0)
    keys = (probe_owner[:, 0] * SENS_DEV + probe_sensor).astype(jnp.int32)
    readings = jax.ops.segment_sum(values, keys, num_segments=N_PX * N_PY * SENS_DEV)
    weighted = readings * sensor_weight
    returned = weighted[keys]
    source = jnp.zeros(flat.shape, jnp.float32).at[global_nodes.reshape(-1)].add((probe_weights * returned[None, :]).reshape(-1))
    adjoint = chebyshev(source.reshape(tangent.shape), permittivity)
    return sensitivity(background_field, adjoint)
```

```python
import functools

import jax
import jax.numpy as jnp
from jax import lax
from jax.experimental import pallas as pl
from jax.experimental.pallas import tpu as pltpu
from jax.sharding import PartitionSpec as P

SWEEPS = 4
STRIP = 8
MESH = pl.DeviceIdType.MESH

bound_low = 1.0
bound_high = 25.0

PERT, BACK, PERMIT, TAN, ADJ = 0, 1, 2, 3, 6
EXCHANGES = 10
SEARCHES = (TAN, ADJ)


def cheb_steps():
    centre = 0.5 * (bound_high + bound_low)
    half_width = 0.5 * (bound_high - bound_low)
    spread = centre / half_width
    ratio = 1.0 / spread
    steps = []
    for _ in range(SWEEPS - 1):
        following = 1.0 / (2.0 * spread - ratio)
        steps.append((following * ratio, 2.0 * following / half_width))
        ratio = following
    return centre, steps


def split_rows(row):
    high = row.astype(jnp.bfloat16).astype(jnp.float32)
    rest = row - high
    middle = rest.astype(jnp.bfloat16).astype(jnp.float32)
    low = rest - middle
    index = lax.broadcasted_iota(jnp.int32, (16, row.shape[1]), 0)
    parts = jnp.where(index == 0, high, jnp.where(index == 1, middle, jnp.where(index == 2, low, 0.0)))
    return parts.astype(jnp.bfloat16)


def kernel(
    n_px, n_py,
    back, pert, permit, nodes, weights, owner, sensor, sensor_weight,
    out,
    search, remain, coef_x, coef_yd, coef_yu, coef_zd, coef_zu, diag,
    halo_x, halo_y, pack_y,
    field_t, row_hot, row_val, z_hot, key_hot, values, sums_py, sums_px,
    send_sem, recv_sem, py_send, py_recv, px_send, px_recv,
):
    rows, cols, depth = back.shape
    strips = cols // STRIP
    last = rows - 1
    probes = nodes.shape[1]
    kinds = nodes.shape[0]
    sensors_dev = sensor_weight.shape[0]
    sensors = key_hot.shape[0]
    nodes_dev = rows * cols
    shift = depth.bit_length() - 1
    assert depth == 1 << shift
    px, py = lax.axis_index("px"), lax.axis_index("py")
    centre, steps = cheb_steps()

    lane = lax.broadcasted_iota(jnp.int32, (STRIP, depth), 1)
    sub = lax.broadcasted_iota(jnp.int32, (STRIP, depth), 0)
    first_lane, last_lane = lane == 0, lane == depth - 1
    first_sub, last_sub = sub == 0, sub == STRIP - 1

    halo_x[...] = jnp.zeros_like(halo_x)
    halo_y[...] = jnp.zeros_like(halo_y)
    for side, face in ((0, 0), (1, last)):
        halo_x[BACK, side] = back[face]
        halo_x[PERMIT, side] = -permit[face]
    for slot, array in ((BACK, back), (PERT, pert), (PERMIT, permit)):
        for x in range(rows):
            for side, face in ((0, 0), (1, cols - 1)):
                row = array[x, face : face + 1, :]
                pack_y[slot, side, x : x + 1, :] = row
                if slot == BACK:
                    halo_y[slot, side, x : x + 1, :] = row
                if slot == PERMIT:
                    halo_y[slot, side, x : x + 1, :] = -row

    barrier = pltpu.get_barrier_semaphore()
    for step in range(1, n_px):
        pl.semaphore_signal(barrier, inc=1, device_id={"px": lax.rem(px + step, n_px)}, device_id_type=MESH)
    for step in range(1, n_py):
        pl.semaphore_signal(barrier, inc=1, device_id={"py": lax.rem(py + step, n_py)}, device_id_type=MESH)
    pl.semaphore_wait(barrier, n_px + n_py - 2)

    def copy(slot, way, array):
        side = way % 2
        if way < 2:
            source = array.at[last if side else 0]
            target = halo_x.at[slot, 1 - side]
            device = {"px": lax.rem(px + (1 if side else n_px - 1), n_px)}
        else:
            source = pack_y.at[slot, side]
            target = halo_y.at[slot, 1 - side]
            device = {"py": lax.rem(py + (1 if side else n_py - 1), n_py)}
        return pltpu.make_async_remote_copy(
            src_ref=source, dst_ref=target, send_sem=send_sem.at[slot, way], recv_sem=recv_sem.at[slot, way],
            device_id=device, device_id_type=MESH,
        )

    sends = (px > 0, px < n_px - 1, py > 0, py < n_py - 1)
    takes = (sends[1], sends[0], sends[3], sends[2])

    def start(slot, way, array):
        @pl.when(sends[way])
        def _():
            copy(slot, way, array).start()

    def finish(slot, ways, array):
        for way in ways:
            @pl.when(takes[way])
            def _():
                copy(slot, way, array).wait_recv()

            @pl.when(sends[way])
            def _():
                copy(slot, way, array).wait_send()

    for slot, array in ((PERT, pert), (BACK, back), (PERMIT, permit)):
        for way in (2, 3, 0, 1):
            start(slot, way, array)

    def hots(kind, _):
        node = nodes[pl.ds(kind, 1), :]
        at_row = lax.shift_right_logical(node, shift)
        at_depth = lax.bitwise_and(node, depth - 1)
        columns = pl.ds(pl.multiple_of(kind * probes, probes), probes)
        index = lax.broadcasted_iota(jnp.int32, (16, probes), 0)

        def row_block(block, _):
            first = pl.multiple_of(block * 16, 16)
            row_hot[pl.ds(first, 16), columns] = jnp.where(index + first == at_row, 1.0, 0.0).astype(jnp.bfloat16)
            return 0

        def z_block(block, _):
            first = pl.multiple_of(block * 16, 16)
            z_hot[pl.ds(first, 16), columns] = jnp.where(index + first == at_depth, 1.0, 0.0).astype(jnp.bfloat16)
            return 0

        lax.fori_loop(0, nodes_dev // 16, row_block, 0)
        lax.fori_loop(0, depth // 16, z_block, 0)
        return 0

    lax.fori_loop(0, kinds, hots, 0)
    key = owner[...] * sensors_dev + sensor[...]
    key_index = lax.broadcasted_iota(jnp.int32, (16, probes), 0)

    def key_block(block, _):
        first = pl.multiple_of(block * 16, 16)
        key_hot[pl.ds(first, 16), :] = jnp.where(key_index + first == key, 1.0, 0.0).astype(jnp.bfloat16)
        return 0

    lax.fori_loop(0, sensors // 16, key_block, 0)

    def around(array, below, above, slot, x, strip):
        y = strip * STRIP
        here = array[x, y : y + STRIP, :]
        xd, xu = below[y : y + STRIP, :], above[y : y + STRIP, :]
        before = array[x, y - 1 : y, :] if strip > 0 else halo_y[slot, 0, pl.ds(x, 1), :]
        after = array[x, y + STRIP : y + STRIP + 1, :] if strip < strips - 1 else halo_y[slot, 1, pl.ds(x, 1), :]
        yd = jnp.where(first_sub, before, pltpu.roll(here, 1, 0))
        yu = jnp.where(last_sub, after, pltpu.roll(here, STRIP - 1, 0))
        zd, zu = pltpu.roll(here, 1, 1), pltpu.roll(here, depth - 1, 1)
        return here, (xd, xu, yd, yu, zd, zu)

    def planes(plane, slots, arrays, after_face):
        for slot, array in zip(slots, arrays):
            finish(slot, (2, 3), array)

        def inner(x, _):
            plane(x, [a.at[x - 1] for a in arrays], [a.at[x + 1] for a in arrays])
            return 0

        lax.fori_loop(1, last, inner, 0)
        for slot, array in zip(slots, arrays):
            finish(slot, (0, 1), array)
        plane(0, [halo_x.at[s, 0] for s in slots], [a.at[1] for a in arrays])
        after_face(0)
        plane(last, [a.at[last - 1] for a in arrays], [halo_x.at[s, 1] for s in slots])
        after_face(1)

    def send_y(slot, array):
        for x in range(rows):
            for side, face in ((0, 0), (1, cols - 1)):
                pack_y[slot, side, x : x + 1, :] = array[x, face : face + 1, :]
        start(slot, 2, array)
        start(slot, 3, array)

    def source_plane(x, below, above):
        for strip in range(strips):
            y = strip * STRIP
            c, c_near = around(pert, below[0], above[0], PERT, x, strip)
            f, f_near = around(back, below[1], above[1], BACK, x, strip)
            terms = [(c + cn) * (fn - f) for cn, fn in zip(c_near, f_near)]
            total = terms[0] + terms[1] + terms[2] + terms[3]
            total = total + jnp.where(first_lane, 0.0, terms[4]) + jnp.where(last_lane, 0.0, terms[5])
            total = 0.5 * total
            remain[x, y : y + STRIP, :] = total
            search[0, x, y : y + STRIP, :] = total / centre

    planes(source_plane, (PERT, BACK), (pert, back), lambda side: start(TAN, side, search.at[0]))
    send_y(TAN, search.at[0])

    def coef_plane(x, below, above):
        for strip in range(strips):
            y = strip * STRIP
            c, (xd, xu, yd, yu, zd, zu) = around(permit, below[0], above[0], PERMIT, x, strip)
            xd, xu, yd, yu = 0.5 * (c + xd), 0.5 * (c + xu), 0.5 * (c + yd), 0.5 * (c + yu)
            zd = jnp.where(first_lane, 0.0, 0.5 * (c + zd))
            zu = jnp.where(last_lane, 0.0, 0.5 * (c + zu))
            coef_x[x, y : y + STRIP, :] = xd
            if isinstance(x, int) and x == last:
                coef_x[rows, y : y + STRIP, :] = xu
            coef_yd[x, y : y + STRIP, :] = yd
            coef_yu[x, y : y + STRIP, :] = yu
            coef_zd[x, y : y + STRIP, :] = zd
            coef_zu[x, y : y + STRIP, :] = zu
            diag[x, y : y + STRIP, :] = 1.0 + ((xd + xu) + (yd + yu) + (zd + zu))

    planes(coef_plane, (PERMIT,), (permit,), lambda side: None)

    def solve(first):
        for sweep, (keep, gain) in enumerate(steps):
            slot = first + sweep
            now, later = search.at[sweep], search.at[sweep + 1]
            sent = sweep < SWEEPS - 2 or first == ADJ

            def sweep_plane(x, below, above):
                for strip in range(strips):
                    y = strip * STRIP
                    at = (x, slice(y, y + STRIP))
                    f, (xd, xu, yd, yu, zd, zu) = around(now, below[0], above[0], slot, x, strip)
                    off = coef_x[at] * xd + coef_x[x + 1, y : y + STRIP, :] * xu
                    off = off + (coef_yd[at] * yd + coef_yu[at] * yu)
                    off = off + (coef_zd[at] * zd + coef_zu[at] * zu)
                    left = remain[at] - diag[at] * f + off
                    remain[at] = left
                    later[at] = keep * f + gain * left

            def after_face(side):
                if sent:
                    start(slot + 1, side, later)

            planes(sweep_plane, (slot,), (now,), after_face)
            if sent:
                send_y(slot + 1, later)

        def total_plane(x, _):
            for strip in range(strips):
                at = (x, slice(strip * STRIP, (strip + 1) * STRIP))
                total = search[(0,) + at]
                for index in range(1, SWEEPS):
                    total = total + search[(index,) + at]
                remain[at] = total
            return 0

        lax.fori_loop(0, rows, total_plane, 0)

    solve(TAN)

    for x in range(rows):
        turned = remain[x].T
        high = turned.astype(jnp.bfloat16)
        field_t[:, x * cols : (x + 1) * cols] = high
        field_t[:, nodes_dev + x * cols : nodes_dev + (x + 1) * cols] = (turned - high.astype(jnp.float32)).astype(jnp.bfloat16)

    width = probes // 2
    tall = 256
    values[...] = jnp.zeros_like(values)

    def pick(kind, _):
        for half in range(2):
            spot = pl.ds(half * width, width)
            columns = pl.ds(pl.multiple_of(kind * probes + half * width, width), width)
            at_depth = lax.bitwise_and(nodes[pl.ds(kind, 1), spot], depth - 1)
            hot = row_hot[:, columns]
            hot = jnp.concatenate([hot, hot], axis=0)
            index = lax.broadcasted_iota(jnp.int32, (tall, width), 0)
            found = jnp.zeros((1, width), jnp.float32)
            for block in range(depth // tall):
                lines = jnp.dot(field_t[block * tall : (block + 1) * tall, :], hot, preferred_element_type=jnp.float32)
                found = found + jnp.sum(jnp.where(index + block * tall == at_depth, lines, 0.0), axis=0, keepdims=True)
            values[:, spot] += weights[pl.ds(kind, 1), spot] * found
        return 0

    lax.fori_loop(0, kinds, pick, 0)

    contract_lanes = (((1,), (1,)), ((), ()))
    partial = lax.dot_general(split_rows(values[...]), key_hot[...], contract_lanes, preferred_element_type=jnp.float32)
    partial = jnp.sum(partial, axis=0, keepdims=True)
    place = lax.broadcasted_iota(jnp.int32, (1, sensors), 1) - (px * n_py + py) * sensors_dev
    own = jnp.zeros((1, sensors), jnp.float32)
    for index in range(sensors_dev):
        own = jnp.where(place == index, sensor_weight[index], own)
    line = lax.broadcasted_iota(jnp.int32, (8, sensors), 0)
    sums_py[0] = jnp.where(line == 0, partial, jnp.where(line == 1, own, 0.0))

    def all_sum(sums, count, me, axis, sent, got):
        copies = []
        for step in range(1, count):
            move = pltpu.make_async_remote_copy(
                src_ref=sums.at[0], dst_ref=sums.at[step], send_sem=sent.at[step], recv_sem=got.at[step],
                device_id={axis: lax.rem(me + step, count)}, device_id_type=MESH,
            )
            move.start()
            copies.append(move)
        total = sums[0]
        for step, move in enumerate(copies):
            move.wait()
            total = total + sums[step + 1]
        return total

    sums_px[0] = all_sum(sums_py, n_py, py, "py", py_send, py_recv)
    total = all_sum(sums_px, n_px, px, "px", px_send, px_recv)
    weighted = total[0:1] * total[1:2]
    returned = jnp.dot(split_rows(weighted), key_hot[...], preferred_element_type=jnp.float32)
    returned = jnp.sum(returned, axis=0, keepdims=True)

    for kind in range(kinds):
        columns = slice(kind * probes, (kind + 1) * probes)
        value = weights[kind : kind + 1, :] * returned
        high = value.astype(jnp.bfloat16)
        low = (value - high.astype(jnp.float32)).astype(jnp.bfloat16)
        row_val[0:nodes_dev, columns] = row_hot[:, columns] * high
        row_val[nodes_dev:, columns] = row_hot[:, columns] * low

    for block in range(depth // tall):
        span = slice(block * tall, (block + 1) * tall)
        both = lax.dot_general(row_val[...], z_hot[span, :], contract_lanes, preferred_element_type=jnp.float32)
        both = (both[:nodes_dev] + both[nodes_dev:]).reshape(rows, cols, tall)
        remain[:, :, span] = both
        search[0, :, :, span] = both / centre
    start(ADJ, 0, search.at[0])
    start(ADJ, 1, search.at[0])
    send_y(ADJ, search.at[0])

    solve(ADJ)

    end = ADJ + SWEEPS - 1

    def sum_halo(halo, side):
        halo[end, side] = (halo[ADJ, side] + halo[ADJ + 1, side]) + (halo[ADJ + 2, side] + halo[end, side])

    finish(end, (2, 3), search.at[SWEEPS - 1])
    for side in range(2):
        sum_halo(halo_y, side)

    def sense_plane(x, below, above):
        for strip in range(strips):
            y = strip * STRIP
            b, b_near = around(back, below[0], above[0], BACK, x, strip)
            a, a_near = around(remain, below[1], above[1], end, x, strip)
            terms = [(b - bn) * (a - an) for bn, an in zip(b_near, a_near)]
            total = terms[0] + terms[1] + terms[2] + terms[3]
            total = total + jnp.where(first_lane, 0.0, terms[4]) + jnp.where(last_lane, 0.0, terms[5])
            out[x, y : y + STRIP, :] = -0.5 * total

    def inner(x, _):
        sense_plane(x, [back.at[x - 1], remain.at[x - 1]], [back.at[x + 1], remain.at[x + 1]])
        return 0

    lax.fori_loop(1, last, inner, 0)
    finish(end, (0, 1), search.at[SWEEPS - 1])
    for side in range(2):
        sum_halo(halo_x, side)
    sense_plane(0, [halo_x.at[BACK, 0], halo_x.at[end, 0]], [back.at[1], remain.at[1]])
    sense_plane(last, [back.at[last - 1], remain.at[last - 1]], [halo_x.at[BACK, 1], halo_x.at[end, 1]])


def body(back, pert, permit, nodes, weights, owner, sensor, sensor_weight):
    n_px, n_py = lax.axis_size("px"), lax.axis_size("py")
    rows, cols, depth = back.shape
    kinds, probes = nodes.shape
    sensors = sensor_weight.shape[0] * n_px * n_py
    nodes_dev = rows * cols
    f32, bf16 = jnp.float32, jnp.bfloat16
    vmem = pl.BlockSpec(memory_space=pltpu.VMEM)
    smem = pl.BlockSpec(memory_space=pltpu.SMEM)
    block = pltpu.VMEM((rows, cols, depth), f32)
    dma = pltpu.SemaphoreType.DMA
    return pl.pallas_call(
        functools.partial(kernel, n_px, n_py),
        out_shape=jax.ShapeDtypeStruct((rows, cols, depth), f32),
        in_specs=[vmem] * 7 + [smem],
        out_specs=vmem,
        scratch_shapes=[
            pltpu.VMEM((SWEEPS, rows, cols, depth), f32),
            block,
            pltpu.VMEM((rows + 1, cols, depth), f32),
            block, block, block, block, block,
            pltpu.VMEM((EXCHANGES, 2, cols, depth), f32),
            pltpu.VMEM((EXCHANGES, 2, rows, depth), f32),
            pltpu.VMEM((EXCHANGES, 2, rows, depth), f32),
            pltpu.VMEM((depth, 2 * nodes_dev), bf16),
            pltpu.VMEM((nodes_dev, kinds * probes), bf16),
            pltpu.VMEM((2 * nodes_dev, kinds * probes), bf16),
            pltpu.VMEM((depth, kinds * probes), bf16),
            pltpu.VMEM((sensors, probes), bf16),
            pltpu.VMEM((1, probes), f32),
            pltpu.VMEM((n_py, 8, sensors), f32),
            pltpu.VMEM((n_px, 8, sensors), f32),
            dma((EXCHANGES, 4)), dma((EXCHANGES, 4)),
            dma((n_py,)), dma((n_py,)), dma((n_px,)), dma((n_px,)),
        ],
        compiler_params=pltpu.CompilerParams(
            collective_id=0, has_side_effects=True, vmem_limit_bytes=56 * 1024 * 1024
        ),
        cost_estimate=pl.CostEstimate(flops=10_000_000_000, bytes_accessed=4_500_000, transcendentals=0),
    )(
        back, pert, permit, nodes, weights, owner.reshape(1, probes), sensor.reshape(1, probes), sensor_weight
    )


def solution(mesh):
    placed = (
        P("px", "py", None),
        P("px", "py", None),
        P("px", "py", None),
        P(None, ("px", "py")),
        P(None, ("px", "py")),
        P(("px", "py"), None),
        P(("px", "py")),
        P(("px", "py")),
    )
    return jax.shard_map(
        body, mesh=mesh, in_specs=placed, out_specs=P("px", "py", None), check_vma=False
    )
```

```python
import functools

import jax
import jax.numpy as jnp
from jax import lax
from jax.experimental import pallas as pl
from jax.experimental.pallas import tpu as pltpu
from jax.sharding import PartitionSpec as P

SWEEPS = 4
STRIP = 8
MESH = pl.DeviceIdType.MESH

bound_low = 1.0
bound_high = 25.0

PERT, BACK, PERMIT, TAN, ADJ = 0, 1, 2, 3, 6
EXCHANGES = 10


def cheb_steps():
    centre = 0.5 * (bound_high + bound_low)
    half_width = 0.5 * (bound_high - bound_low)
    spread = centre / half_width
    ratio = 1.0 / spread
    steps = []
    for _ in range(SWEEPS - 1):
        following = 1.0 / (2.0 * spread - ratio)
        steps.append((following * ratio, 2.0 * following / half_width))
        ratio = following
    return centre, steps


def split_rows(row):
    high = row.astype(jnp.bfloat16).astype(jnp.float32)
    rest = row - high
    middle = rest.astype(jnp.bfloat16).astype(jnp.float32)
    low = rest - middle
    index = lax.broadcasted_iota(jnp.int32, (16, row.shape[1]), 0)
    parts = jnp.where(index == 0, high, jnp.where(index == 1, middle, jnp.where(index == 2, low, 0.0)))
    return parts.astype(jnp.bfloat16)


def kernel(
    n_px, n_py,
    back, pert, permit, nodes, weights, owner, sensor, sensor_weight,
    out,
    search, remain, coef_x, coef_yd, coef_yu, coef_zd, coef_zu, diag,
    halo_x, halo_y, pack_y,
    field_t, row_hot, row_val, z_hot, key_hot, values, sums_py, sums_px,
    x_send, x_recv, y_send, y_recv, py_send, py_recv, px_send, px_recv,
):
    rows, cols, depth = back.shape
    strips = cols // STRIP
    last = rows - 1
    probes = nodes.shape[1]
    kinds = nodes.shape[0]
    sensors_dev = sensor_weight.shape[0]
    sensors = key_hot.shape[0]
    nodes_dev = rows * cols
    shift = depth.bit_length() - 1
    assert depth == 1 << shift
    px, py = lax.axis_index("px"), lax.axis_index("py")
    centre, steps = cheb_steps()

    lane = lax.broadcasted_iota(jnp.int32, (STRIP, depth), 1)
    sub = lax.broadcasted_iota(jnp.int32, (STRIP, depth), 0)
    first_lane, last_lane = lane == 0, lane == depth - 1
    first_sub, last_sub = sub == 0, sub == STRIP - 1

    halo_x[...] = jnp.zeros_like(halo_x)
    halo_y[...] = jnp.zeros_like(halo_y)
    pack_y[...] = jnp.zeros_like(pack_y)
    for side, face in ((0, 0), (1, last)):
        halo_x[BACK, side] = back[face]
        halo_x[PERMIT, side] = -permit[face]
    for slot, array in ((BACK, back), (PERT, pert), (PERMIT, permit)):
        for x in range(rows):
            for side, face in ((0, 0), (1, cols - 1)):
                row = array[x, face : face + 1, :]
                pack_y[slot, 0, side, x : x + 1, :] = row
                if slot == BACK:
                    halo_y[slot, 0, side, x : x + 1, :] = row
                if slot == PERMIT:
                    halo_y[slot, 0, side, x : x + 1, :] = -row

    barrier = pltpu.get_barrier_semaphore()
    for step in range(1, n_px):
        pl.semaphore_signal(barrier, inc=1, device_id={"px": lax.rem(px + step, n_px)}, device_id_type=MESH)
    for step in range(1, n_py):
        pl.semaphore_signal(barrier, inc=1, device_id={"py": lax.rem(py + step, n_py)}, device_id_type=MESH)
    pl.semaphore_wait(barrier, n_px + n_py - 2)

    def copy_x(slot, side, strip, array):
        span = pl.ds(strip * STRIP, STRIP)
        return pltpu.make_async_remote_copy(
            src_ref=array.at[last if side else 0, span], dst_ref=halo_x.at[slot, 1 - side, span],
            send_sem=x_send.at[slot, side, strip], recv_sem=x_recv.at[slot, side, strip],
            device_id={"px": lax.rem(px + (1 if side else n_px - 1), n_px)}, device_id_type=MESH,
        )

    def copy_y(slot, side, part):
        return pltpu.make_async_remote_copy(
            src_ref=pack_y.at[slot, part, side], dst_ref=halo_y.at[slot, part, 1 - side],
            send_sem=y_send.at[slot, side, part], recv_sem=y_recv.at[slot, side, part],
            device_id={"py": lax.rem(py + (1 if side else n_py - 1), n_py)}, device_id_type=MESH,
        )

    has_x = (px > 0, px < n_px - 1)
    has_y = (py > 0, py < n_py - 1)
    order = (0, strips - 1) + tuple(range(1, strips - 1))

    def start_x(slot, strip, array):
        for side in range(2):
            pl.when(has_x[side])(lambda: copy_x(slot, side, strip, array).start())

    def start_y(slot, side, part):
        pl.when(has_y[side])(lambda: copy_y(slot, side, part).start())

    def take_x(slot, strip, array):
        for side in range(2):
            pl.when(has_x[1 - side])(lambda: copy_x(slot, side, strip, array).wait_recv())

    def take_y(slot, side, part):
        pl.when(has_y[side])(lambda: copy_y(slot, 1 - side, part).wait_recv())

    def sent(slot, parts, array):
        for side in range(2):
            @pl.when(has_x[side])
            def _():
                for strip in range(strips):
                    copy_x(slot, side, strip, array).wait_send()

            @pl.when(has_y[side])
            def _():
                for part in parts:
                    copy_y(slot, side, part).wait_send()

    fields = ((PERT, pert), (BACK, back), (PERMIT, permit))
    for slot, _ in fields:
        for side in range(2):
            start_y(slot, side, 0)
    for strip in order:
        for slot, array in fields[:2]:
            start_x(slot, strip, array)
    for strip in order:
        start_x(PERMIT, strip, permit)

    def hots(kind, _):
        node = nodes[pl.ds(kind, 1), :]
        at_row = lax.shift_right_logical(node, shift)
        at_depth = lax.bitwise_and(node, depth - 1)
        columns = pl.ds(pl.multiple_of(kind * probes, probes), probes)
        index = lax.broadcasted_iota(jnp.int32, (16, probes), 0)

        def row_block(block, _):
            first = pl.multiple_of(block * 16, 16)
            row_hot[pl.ds(first, 16), columns] = jnp.where(index + first == at_row, 1.0, 0.0).astype(jnp.bfloat16)
            return 0

        def z_block(block, _):
            first = pl.multiple_of(block * 16, 16)
            z_hot[pl.ds(first, 16), columns] = jnp.where(index + first == at_depth, 1.0, 0.0).astype(jnp.bfloat16)
            return 0

        lax.fori_loop(0, nodes_dev // 16, row_block, 0)
        lax.fori_loop(0, depth // 16, z_block, 0)
        return 0

    lax.fori_loop(0, kinds, hots, 0)
    key = owner[...] * sensors_dev + sensor[...]
    key_index = lax.broadcasted_iota(jnp.int32, (16, probes), 0)

    def key_block(block, _):
        first = pl.multiple_of(block * 16, 16)
        key_hot[pl.ds(first, 16), :] = jnp.where(key_index + first == key, 1.0, 0.0).astype(jnp.bfloat16)
        return 0

    lax.fori_loop(0, sensors // 16, key_block, 0)

    def around(array, below, above, slot, x, strip):
        y = strip * STRIP
        part = 1 if slot >= TAN and isinstance(x, int) else 0
        here = array[x, y : y + STRIP, :]
        xd, xu = below[y : y + STRIP, :], above[y : y + STRIP, :]
        before = array[x, y - 1 : y, :] if strip > 0 else halo_y[slot, part, 0, pl.ds(x, 1), :]
        after = array[x, y + STRIP : y + STRIP + 1, :] if strip < strips - 1 else halo_y[slot, part, 1, pl.ds(x, 1), :]
        yd = jnp.where(first_sub, before, pltpu.roll(here, 1, 0))
        yu = jnp.where(last_sub, after, pltpu.roll(here, STRIP - 1, 0))
        zd, zu = pltpu.roll(here, 1, 1), pltpu.roll(here, depth - 1, 1)
        return here, (xd, xu, yd, yu, zd, zu)

    def inner_planes(work, slots, arrays):
        for slot in slots:
            take_y(slot, 0, 0)
            take_y(slot, 1, 0)

        def step(x, _):
            for strip in range(strips):
                work(x, strip, [a.at[x - 1] for a in arrays], [a.at[x + 1] for a in arrays])
            return 0

        lax.fori_loop(1, last, step, 0)

    def outer_planes(work, slots, arrays, after):
        for strip in order:
            for slot, array in zip(slots, arrays):
                take_x(slot, strip, array)
                if slot >= TAN:
                    for side, edge in ((0, 0), (1, strips - 1)):
                        if strip == edge:
                            take_y(slot, side, 1)
            work(0, strip, [halo_x.at[s, 0] for s in slots], [a.at[1] for a in arrays])
            work(last, strip, [a.at[last - 1] for a in arrays], [halo_x.at[s, 1] for s in slots])
            after(strip)

    def nothing(strip):
        return None

    def send_inner(slot, array):
        for side, face in ((0, 0), (1, cols - 1)):
            for x in range(1, last):
                pack_y[slot, 0, side, x : x + 1, :] = array[x, face : face + 1, :]
            start_y(slot, side, 0)

    def send_outer(slot, array):
        def after(strip):
            start_x(slot, strip, array)
            for side, edge, face in ((0, 0, 0), (1, strips - 1, cols - 1)):
                if strip == edge:
                    for x in (0, last):
                        pack_y[slot, 1, side, x : x + 1, :] = array[x, face : face + 1, :]
                    start_y(slot, side, 1)

        return after

    def source_work(x, strip, below, above):
        y = strip * STRIP
        c, c_near = around(pert, below[0], above[0], PERT, x, strip)
        f, f_near = around(back, below[1], above[1], BACK, x, strip)
        terms = [(c + cn) * (fn - f) for cn, fn in zip(c_near, f_near)]
        total = terms[0] + terms[1] + terms[2] + terms[3]
        total = total + jnp.where(first_lane, 0.0, terms[4]) + jnp.where(last_lane, 0.0, terms[5])
        total = 0.5 * total
        remain[x, y : y + STRIP, :] = total
        search[0, x, y : y + STRIP, :] = total / centre

    def coef_work(x, strip, below, above):
        y = strip * STRIP
        c, (xd, xu, yd, yu, zd, zu) = around(permit, below[0], above[0], PERMIT, x, strip)
        xd, xu, yd, yu = 0.5 * (c + xd), 0.5 * (c + xu), 0.5 * (c + yd), 0.5 * (c + yu)
        zd = jnp.where(first_lane, 0.0, 0.5 * (c + zd))
        zu = jnp.where(last_lane, 0.0, 0.5 * (c + zu))
        coef_x[x, y : y + STRIP, :] = xd
        if isinstance(x, int) and x == last:
            coef_x[rows, y : y + STRIP, :] = xu
        coef_yd[x, y : y + STRIP, :] = yd
        coef_yu[x, y : y + STRIP, :] = yu
        coef_zd[x, y : y + STRIP, :] = zd
        coef_zu[x, y : y + STRIP, :] = zu
        diag[x, y : y + STRIP, :] = 1.0 + ((xd + xu) + (yd + yu) + (zd + zu))

    inner_planes(source_work, (PERT, BACK), (pert, back))
    send_inner(TAN, search.at[0])
    inner_planes(coef_work, (PERMIT,), (permit,))
    outer_planes(source_work, (PERT, BACK), (pert, back), send_outer(TAN, search.at[0]))
    outer_planes(coef_work, (PERMIT,), (permit,), nothing)
    for slot, array in fields:
        sent(slot, (0,), array)

    def solve(first):
        for sweep, (keep, gain) in enumerate(steps):
            slot = first + sweep
            now, later = search.at[sweep], search.at[sweep + 1]
            more = sweep < SWEEPS - 2 or first == ADJ

            def sweep_work(x, strip, below, above):
                y = strip * STRIP
                at = (x, slice(y, y + STRIP))
                f, (xd, xu, yd, yu, zd, zu) = around(now, below[0], above[0], slot, x, strip)
                off = coef_x[at] * xd + coef_x[x + 1, y : y + STRIP, :] * xu
                off = off + (coef_yd[at] * yd + coef_yu[at] * yu)
                off = off + (coef_zd[at] * zd + coef_zu[at] * zu)
                left = remain[at] - diag[at] * f + off
                remain[at] = left
                later[at] = keep * f + gain * left

            inner_planes(sweep_work, (slot,), (now,))
            if more:
                send_inner(slot + 1, later)
            outer_planes(sweep_work, (slot,), (now,), send_outer(slot + 1, later) if more else nothing)
            sent(slot, (0, 1), now)

        def total_plane(x, _):
            for strip in range(strips):
                at = (x, slice(strip * STRIP, (strip + 1) * STRIP))
                total = search[(0,) + at]
                for index in range(1, SWEEPS):
                    total = total + search[(index,) + at]
                remain[at] = total
            return 0

        lax.fori_loop(0, rows, total_plane, 0)

    solve(TAN)

    group = 128 // cols
    for part in range(rows // group):
        turned = remain[part * group : (part + 1) * group].reshape(128, depth).T
        high = turned.astype(jnp.bfloat16)
        field_t[:, part * 128 : (part + 1) * 128] = high
        field_t[:, nodes_dev + part * 128 : nodes_dev + (part + 1) * 128] = (turned - high.astype(jnp.float32)).astype(jnp.bfloat16)

    width = probes // 2
    tall = 256
    values[...] = jnp.zeros_like(values)
    index = lax.broadcasted_iota(jnp.int32, (depth, width), 0)

    def pick(kind, _):
        for half in range(2):
            spot = pl.ds(half * width, width)
            columns = pl.ds(pl.multiple_of(kind * probes + half * width, width), width)
            at_depth = lax.bitwise_and(nodes[pl.ds(kind, 1), spot], depth - 1)
            hot = row_hot[:, columns]
            hot = jnp.concatenate([hot, hot], axis=0)
            lines = jnp.dot(field_t[...], hot, preferred_element_type=jnp.float32)
            found = jnp.sum(jnp.where(index == at_depth, lines, 0.0), axis=0, keepdims=True)
            values[:, spot] += weights[pl.ds(kind, 1), spot] * found
        return 0

    lax.fori_loop(0, kinds, pick, 0)

    contract_lanes = (((1,), (1,)), ((), ()))
    partial = lax.dot_general(split_rows(values[...]), key_hot[...], contract_lanes, preferred_element_type=jnp.float32)
    partial = jnp.sum(partial, axis=0, keepdims=True)
    place = lax.broadcasted_iota(jnp.int32, (1, sensors), 1) - (px * n_py + py) * sensors_dev
    own = jnp.zeros((1, sensors), jnp.float32)
    for index in range(sensors_dev):
        own = jnp.where(place == index, sensor_weight[index], own)
    line = lax.broadcasted_iota(jnp.int32, (8, sensors), 0)
    sums_py[0] = jnp.where(line == 0, partial, jnp.where(line == 1, own, 0.0))

    def all_sum(sums, count, me, axis, sent, got):
        copies = []
        for step in range(1, count):
            move = pltpu.make_async_remote_copy(
                src_ref=sums.at[0], dst_ref=sums.at[step], send_sem=sent.at[step], recv_sem=got.at[step],
                device_id={axis: lax.rem(me + step, count)}, device_id_type=MESH,
            )
            move.start()
            copies.append(move)
        total = sums[0]
        for step, move in enumerate(copies):
            move.wait()
            total = total + sums[step + 1]
        return total

    sums_px[0] = all_sum(sums_py, n_py, py, "py", py_send, py_recv)
    total = all_sum(sums_px, n_px, px, "px", px_send, px_recv)
    weighted = total[0:1] * total[1:2]
    returned = jnp.dot(split_rows(weighted), key_hot[...], preferred_element_type=jnp.float32)
    returned = jnp.sum(returned, axis=0, keepdims=True)

    for kind in range(kinds):
        columns = slice(kind * probes, (kind + 1) * probes)
        value = weights[kind : kind + 1, :] * returned
        high = value.astype(jnp.bfloat16)
        low = (value - high.astype(jnp.float32)).astype(jnp.bfloat16)
        row_val[0:nodes_dev, columns] = row_hot[:, columns] * high
        row_val[nodes_dev:, columns] = row_hot[:, columns] * low

    for block in range(depth // tall):
        span = slice(block * tall, (block + 1) * tall)
        both = lax.dot_general(row_val[...], z_hot[span, :], contract_lanes, preferred_element_type=jnp.float32)
        both = (both[:nodes_dev] + both[nodes_dev:]).reshape(rows, cols, tall)
        remain[:, :, span] = both
        search[0, :, :, span] = both / centre
    for strip in order:
        send_outer(ADJ, search.at[0])(strip)
    send_inner(ADJ, search.at[0])

    solve(ADJ)

    end = ADJ + SWEEPS - 1

    def sum_halo(halo, at):
        halo[(end,) + at] = (halo[(ADJ,) + at] + halo[(ADJ + 1,) + at]) + (halo[(ADJ + 2,) + at] + halo[(end,) + at])

    def sense_work(x, strip, below, above):
        y = strip * STRIP
        b, b_near = around(back, below[0], above[0], BACK, x, strip)
        a, a_near = around(remain, below[1], above[1], end, x, strip)
        terms = [(b - bn) * (a - an) for bn, an in zip(b_near, a_near)]
        total = terms[0] + terms[1] + terms[2] + terms[3]
        total = total + jnp.where(first_lane, 0.0, terms[4]) + jnp.where(last_lane, 0.0, terms[5])
        out[x, y : y + STRIP, :] = total

    def sum_strip(strip):
        for side, edge in ((0, 0), (1, strips - 1)):
            sum_halo(halo_x, (side, slice(strip * STRIP, (strip + 1) * STRIP)))
            if strip == edge:
                sum_halo(halo_y, (1, side))

    newest = search.at[SWEEPS - 1]
    for side in range(2):
        take_y(end, side, 0)
        sum_halo(halo_y, (0, side))
    inner_planes(sense_work, (), (back, remain))
    for strip in order:
        take_x(end, strip, newest)
        for side, edge in ((0, 0), (1, strips - 1)):
            if strip == edge:
                take_y(end, side, 1)
        sum_strip(strip)
        sense_work(0, strip, [halo_x.at[BACK, 0], halo_x.at[end, 0]], [back.at[1], remain.at[1]])
        sense_work(last, strip, [back.at[last - 1], remain.at[last - 1]], [halo_x.at[BACK, 1], halo_x.at[end, 1]])
    sent(end, (0, 1), newest)


def body(back, pert, permit, nodes, weights, owner, sensor, sensor_weight):
    n_px, n_py = lax.axis_size("px"), lax.axis_size("py")
    rows, cols, depth = back.shape
    kinds, probes = nodes.shape
    sensors = sensor_weight.shape[0] * n_px * n_py
    nodes_dev = rows * cols
    f32, bf16 = jnp.float32, jnp.bfloat16
    vmem = pl.BlockSpec(memory_space=pltpu.VMEM)
    smem = pl.BlockSpec(memory_space=pltpu.SMEM)
    block = pltpu.VMEM((rows, cols, depth), f32)
    dma = pltpu.SemaphoreType.DMA
    doubled = pl.pallas_call(
        functools.partial(kernel, n_px, n_py),
        out_shape=jax.ShapeDtypeStruct((rows, cols, depth), f32),
        in_specs=[vmem] * 7 + [smem],
        out_specs=vmem,
        scratch_shapes=[
            pltpu.VMEM((SWEEPS, rows, cols, depth), f32),
            block,
            pltpu.VMEM((rows + 1, cols, depth), f32),
            block, block, block, block, block,
            pltpu.VMEM((EXCHANGES, 2, cols, depth), f32),
            pltpu.VMEM((EXCHANGES, 2, 2, rows, depth), f32),
            pltpu.VMEM((EXCHANGES, 2, 2, rows, depth), f32),
            pltpu.VMEM((depth, 2 * nodes_dev), bf16),
            pltpu.VMEM((nodes_dev, kinds * probes), bf16),
            pltpu.VMEM((2 * nodes_dev, kinds * probes), bf16),
            pltpu.VMEM((depth, kinds * probes), bf16),
            pltpu.VMEM((sensors, probes), bf16),
            pltpu.VMEM((1, probes), f32),
            pltpu.VMEM((n_py, 8, sensors), f32),
            pltpu.VMEM((n_px, 8, sensors), f32),
            dma((EXCHANGES, 2, cols // STRIP)), dma((EXCHANGES, 2, cols // STRIP)),
            dma((EXCHANGES, 2, 2)), dma((EXCHANGES, 2, 2)),
            dma((n_py,)), dma((n_py,)), dma((n_px,)), dma((n_px,)),
        ],
        compiler_params=pltpu.CompilerParams(
            collective_id=0, has_side_effects=True, vmem_limit_bytes=56 * 1024 * 1024
        ),
        cost_estimate=pl.CostEstimate(flops=10_000_000_000, bytes_accessed=4_500_000, transcendentals=0),
    )(
        back, pert, permit, nodes, weights, owner.reshape(1, probes), sensor.reshape(1, probes), sensor_weight
    )
    return -0.5 * doubled


def solution(mesh):
    placed = (
        P("px", "py", None),
        P("px", "py", None),
        P("px", "py", None),
        P(None, ("px", "py")),
        P(None, ("px", "py")),
        P(("px", "py"), None),
        P(("px", "py")),
        P(("px", "py")),
    )
    return jax.shard_map(
        body, mesh=mesh, in_specs=placed, out_specs=P("px", "py", None), check_vma=False
    )
```

```python
import functools

import jax
import jax.numpy as jnp
from jax import lax
from jax.experimental import pallas as pl
from jax.experimental.pallas import tpu as pltpu
from jax.sharding import PartitionSpec as P

SWEEPS = 4
STRIP = 8
MESH = pl.DeviceIdType.MESH

bound_low = 1.0
bound_high = 25.0

PERT, BACK, PERMIT, TAN, ADJ = 0, 1, 2, 3, 6
EXCHANGES = 10


def cheb_steps():
    centre = 0.5 * (bound_high + bound_low)
    half_width = 0.5 * (bound_high - bound_low)
    spread = centre / half_width
    ratio = 1.0 / spread
    steps = []
    for _ in range(SWEEPS - 1):
        following = 1.0 / (2.0 * spread - ratio)
        steps.append((following * ratio, 2.0 * following / half_width))
        ratio = following
    return centre, steps


def split_rows(row):
    high = row.astype(jnp.bfloat16).astype(jnp.float32)
    rest = row - high
    middle = rest.astype(jnp.bfloat16).astype(jnp.float32)
    low = rest - middle
    index = lax.broadcasted_iota(jnp.int32, (16, row.shape[1]), 0)
    parts = jnp.where(index == 0, high, jnp.where(index == 1, middle, jnp.where(index == 2, low, 0.0)))
    return parts.astype(jnp.bfloat16)


def kernel(
    n_px, n_py,
    back, pert, permit, nodes, weights, owner, sensor, sensor_weight,
    out,
    search, remain, coef_x, coef_yd, coef_yu, coef_zd, coef_zu, diag,
    halo_x, halo_y, pack_y,
    field_t, row_hot, row_val, z_hot, key_hot, values, sums_py, sums_px,
    x_send, x_recv, y_send, y_recv, py_send, py_recv, px_send, px_recv,
):
    rows, cols, depth = back.shape
    strips = cols // STRIP
    last = rows - 1
    probes = nodes.shape[1]
    kinds = nodes.shape[0]
    sensors_dev = sensor_weight.shape[0]
    sensors = key_hot.shape[0]
    nodes_dev = rows * cols
    shift = depth.bit_length() - 1
    assert depth == 1 << shift
    px, py = lax.axis_index("px"), lax.axis_index("py")
    centre, steps = cheb_steps()

    lane = lax.broadcasted_iota(jnp.int32, (STRIP, depth), 1)
    sub = lax.broadcasted_iota(jnp.int32, (STRIP, depth), 0)
    first_lane, last_lane = lane == 0, lane == depth - 1
    first_sub, last_sub = sub == 0, sub == STRIP - 1

    halo_x[...] = jnp.zeros_like(halo_x)
    halo_y[...] = jnp.zeros_like(halo_y)
    for side, face in ((0, 0), (1, last)):
        halo_x[BACK, side] = back[face]
        halo_x[PERMIT, side] = -permit[face]
    for slot, array in ((BACK, back), (PERT, pert), (PERMIT, permit)):
        for x in range(rows):
            for side, face in ((0, 0), (1, cols - 1)):
                row = array[x, face : face + 1, :]
                pack_y[slot, 0, side, x : x + 1, :] = row
                if slot == BACK:
                    halo_y[slot, 0, side, x : x + 1, :] = row
                if slot == PERMIT:
                    halo_y[slot, 0, side, x : x + 1, :] = -row

    barrier = pltpu.get_barrier_semaphore()
    for step in range(1, n_px):
        pl.semaphore_signal(barrier, inc=1, device_id={"px": lax.rem(px + step, n_px)}, device_id_type=MESH)
    for step in range(1, n_py):
        pl.semaphore_signal(barrier, inc=1, device_id={"py": lax.rem(py + step, n_py)}, device_id_type=MESH)
    pl.semaphore_wait(barrier, n_px + n_py - 2)

    def copy_x(slot, side, strip, array):
        span = pl.ds(strip * STRIP, STRIP)
        return pltpu.make_async_remote_copy(
            src_ref=array.at[last if side else 0, span], dst_ref=halo_x.at[slot, 1 - side, span],
            send_sem=x_send.at[slot, side, strip], recv_sem=x_recv.at[slot, side, strip],
            device_id={"px": lax.rem(px + (1 if side else n_px - 1), n_px)}, device_id_type=MESH,
        )

    def copy_y(slot, side, part):
        return pltpu.make_async_remote_copy(
            src_ref=pack_y.at[slot, part, side], dst_ref=halo_y.at[slot, part, 1 - side],
            send_sem=y_send.at[slot, side, part], recv_sem=y_recv.at[slot, side, part],
            device_id={"py": lax.rem(py + (1 if side else n_py - 1), n_py)}, device_id_type=MESH,
        )

    has_x = (px > 0, px < n_px - 1)
    has_y = (py > 0, py < n_py - 1)
    order = (0, strips - 1) + tuple(range(1, strips - 1))

    def start_x(slot, strip, array):
        for side in range(2):
            pl.when(has_x[side])(lambda: copy_x(slot, side, strip, array).start())

    def start_y(slot, side, part):
        pl.when(has_y[side])(lambda: copy_y(slot, side, part).start())

    def take_x(slot, strip, array):
        for side in range(2):
            pl.when(has_x[1 - side])(lambda: copy_x(slot, side, strip, array).wait_recv())

    def take_y(slot, side, part):
        pl.when(has_y[side])(lambda: copy_y(slot, 1 - side, part).wait_recv())

    def sent(slot, parts, array):
        for side in range(2):
            @pl.when(has_x[side])
            def _():
                for strip in range(strips):
                    copy_x(slot, side, strip, array).wait_send()

            @pl.when(has_y[side])
            def _():
                for part in parts:
                    copy_y(slot, side, part).wait_send()

    fields = ((PERT, pert), (BACK, back), (PERMIT, permit))
    for slot, _ in fields:
        for side in range(2):
            start_y(slot, side, 0)
    for strip in order:
        for slot, array in fields[:2]:
            start_x(slot, strip, array)
    for strip in order:
        start_x(PERMIT, strip, permit)

    pack_y[TAN:] = jnp.zeros((EXCHANGES - TAN,) + pack_y.shape[1:], jnp.float32)

    def hots(kind, _):
        node = nodes[pl.ds(kind, 1), :]
        at_row = lax.shift_right_logical(node, shift)
        at_depth = lax.bitwise_and(node, depth - 1)
        columns = pl.ds(pl.multiple_of(kind * probes, probes), probes)
        index = lax.broadcasted_iota(jnp.int32, (16, probes), 0)

        def row_block(block, _):
            first = pl.multiple_of(block * 16, 16)
            row_hot[pl.ds(first, 16), columns] = jnp.where(index + first == at_row, 1.0, 0.0).astype(jnp.bfloat16)
            return 0

        def z_block(block, _):
            first = pl.multiple_of(block * 16, 16)
            z_hot[pl.ds(first, 16), columns] = jnp.where(index + first == at_depth, 1.0, 0.0).astype(jnp.bfloat16)
            return 0

        lax.fori_loop(0, nodes_dev // 16, row_block, 0)
        lax.fori_loop(0, depth // 16, z_block, 0)
        return 0

    lax.fori_loop(0, kinds, hots, 0)
    key = owner[...] * sensors_dev + sensor[...]
    key_index = lax.broadcasted_iota(jnp.int32, (16, probes), 0)

    def key_block(block, _):
        first = pl.multiple_of(block * 16, 16)
        key_hot[pl.ds(first, 16), :] = jnp.where(key_index + first == key, 1.0, 0.0).astype(jnp.bfloat16)
        return 0

    lax.fori_loop(0, sensors // 16, key_block, 0)

    def around(array, below, above, slot, x, strip):
        y = strip * STRIP
        part = 1 if slot >= TAN and isinstance(x, int) else 0
        here = array[x, y : y + STRIP, :]
        xd, xu = below[y : y + STRIP, :], above[y : y + STRIP, :]
        before = array[x, y - 1 : y, :] if strip > 0 else halo_y[slot, part, 0, pl.ds(x, 1), :]
        after = array[x, y + STRIP : y + STRIP + 1, :] if strip < strips - 1 else halo_y[slot, part, 1, pl.ds(x, 1), :]
        yd = jnp.where(first_sub, before, pltpu.roll(here, 1, 0))
        yu = jnp.where(last_sub, after, pltpu.roll(here, STRIP - 1, 0))
        zd, zu = pltpu.roll(here, 1, 1), pltpu.roll(here, depth - 1, 1)
        return here, (xd, xu, yd, yu, zd, zu)

    def inner_planes(work, slots, arrays):
        for slot in slots:
            take_y(slot, 0, 0)
            take_y(slot, 1, 0)

        def step(x, _):
            for strip in range(strips):
                work(x, strip, [a.at[x - 1] for a in arrays], [a.at[x + 1] for a in arrays])
            return 0

        lax.fori_loop(1, last, step, 0)

    def outer_planes(work, slots, arrays, after):
        for strip in order:
            for slot, array in zip(slots, arrays):
                take_x(slot, strip, array)
                if slot >= TAN:
                    for side, edge in ((0, 0), (1, strips - 1)):
                        if strip == edge:
                            take_y(slot, side, 1)
            work(0, strip, [halo_x.at[s, 0] for s in slots], [a.at[1] for a in arrays])
            work(last, strip, [a.at[last - 1] for a in arrays], [halo_x.at[s, 1] for s in slots])
            after(strip)

    def nothing(strip):
        return None

    def send_inner(slot, array):
        for side, face in ((0, 0), (1, cols - 1)):
            for x in range(1, last):
                pack_y[slot, 0, side, x : x + 1, :] = array[x, face : face + 1, :]
            start_y(slot, side, 0)

    def send_outer(slot, array):
        def after(strip):
            start_x(slot, strip, array)
            for side, edge, face in ((0, 0, 0), (1, strips - 1, cols - 1)):
                if strip == edge:
                    for x in (0, last):
                        pack_y[slot, 1, side, x : x + 1, :] = array[x, face : face + 1, :]
                    start_y(slot, side, 1)

        return after

    def source_work(x, strip, below, above):
        y = strip * STRIP
        c, c_near = around(pert, below[0], above[0], PERT, x, strip)
        f, f_near = around(back, below[1], above[1], BACK, x, strip)
        terms = [(c + cn) * (fn - f) for cn, fn in zip(c_near, f_near)]
        total = terms[0] + terms[1] + terms[2] + terms[3]
        total = total + jnp.where(first_lane, 0.0, terms[4]) + jnp.where(last_lane, 0.0, terms[5])
        total = 0.5 * total
        remain[x, y : y + STRIP, :] = total
        search[0, x, y : y + STRIP, :] = total / centre

    def coef_work(x, strip, below, above):
        y = strip * STRIP
        c, (xd, xu, yd, yu, zd, zu) = around(permit, below[0], above[0], PERMIT, x, strip)
        xd, xu, yd, yu = 0.5 * (c + xd), 0.5 * (c + xu), 0.5 * (c + yd), 0.5 * (c + yu)
        zd = jnp.where(first_lane, 0.0, 0.5 * (c + zd))
        zu = jnp.where(last_lane, 0.0, 0.5 * (c + zu))
        coef_x[x, y : y + STRIP, :] = xd
        if isinstance(x, int) and x == last:
            coef_x[rows, y : y + STRIP, :] = xu
        coef_yd[x, y : y + STRIP, :] = yd
        coef_yu[x, y : y + STRIP, :] = yu
        coef_zd[x, y : y + STRIP, :] = zd
        coef_zu[x, y : y + STRIP, :] = zu
        diag[x, y : y + STRIP, :] = 1.0 + ((xd + xu) + (yd + yu) + (zd + zu))

    inner_planes(source_work, (PERT, BACK), (pert, back))
    send_inner(TAN, search.at[0])
    inner_planes(coef_work, (PERMIT,), (permit,))
    outer_planes(source_work, (PERT, BACK), (pert, back), send_outer(TAN, search.at[0]))
    outer_planes(coef_work, (PERMIT,), (permit,), nothing)
    for slot, array in fields:
        sent(slot, (0,), array)

    def solve(first):
        for sweep, (keep, gain) in enumerate(steps):
            slot = first + sweep
            now, later = search.at[sweep], search.at[sweep + 1]
            more = sweep < SWEEPS - 2 or first == ADJ

            def sweep_work(x, strip, below, above):
                y = strip * STRIP
                at = (x, slice(y, y + STRIP))
                f, (xd, xu, yd, yu, zd, zu) = around(now, below[0], above[0], slot, x, strip)
                off = coef_x[at] * xd + coef_x[x + 1, y : y + STRIP, :] * xu
                off = off + (coef_yd[at] * yd + coef_yu[at] * yu)
                off = off + (coef_zd[at] * zd + coef_zu[at] * zu)
                left = remain[at] - diag[at] * f + off
                new = keep * f + gain * left
                if sweep < SWEEPS - 2:
                    remain[at] = left
                else:
                    left = f + new
                    for index in range(sweep):
                        left = left + search[(index,) + at]
                    remain[at] = left
                if more:
                    later[at] = new

            inner_planes(sweep_work, (slot,), (now,))
            if more:
                send_inner(slot + 1, later)
            outer_planes(sweep_work, (slot,), (now,), send_outer(slot + 1, later) if more else nothing)
            sent(slot, (0, 1), now)

    solve(TAN)

    group = 128 // cols
    for part in range(rows // group):
        turned = remain[part * group : (part + 1) * group].reshape(128, depth).T
        high = turned.astype(jnp.bfloat16)
        field_t[:, part * 128 : (part + 1) * 128] = high
        field_t[:, nodes_dev + part * 128 : nodes_dev + (part + 1) * 128] = (turned - high.astype(jnp.float32)).astype(jnp.bfloat16)

    width = probes // 2
    tall = 256
    values[...] = jnp.zeros_like(values)
    index = lax.broadcasted_iota(jnp.int32, (depth, width), 0)

    def pick(kind, _):
        for half in range(2):
            spot = pl.ds(half * width, width)
            columns = pl.ds(pl.multiple_of(kind * probes + half * width, width), width)
            at_depth = lax.bitwise_and(nodes[pl.ds(kind, 1), spot], depth - 1)
            hot = row_hot[:, columns]
            hot = jnp.concatenate([hot, hot], axis=0)
            lines = jnp.dot(field_t[...], hot, preferred_element_type=jnp.float32)
            found = jnp.sum(jnp.where(index == at_depth, lines, 0.0), axis=0, keepdims=True)
            values[:, spot] += weights[pl.ds(kind, 1), spot] * found
        return 0

    lax.fori_loop(0, kinds, pick, 0)

    contract_lanes = (((1,), (1,)), ((), ()))
    partial = lax.dot_general(split_rows(values[...]), key_hot[...], contract_lanes, preferred_element_type=jnp.float32)
    partial = jnp.sum(partial, axis=0, keepdims=True)
    place = lax.broadcasted_iota(jnp.int32, (1, sensors), 1) - (px * n_py + py) * sensors_dev
    own = jnp.zeros((1, sensors), jnp.float32)
    for index in range(sensors_dev):
        own = jnp.where(place == index, sensor_weight[index], own)
    line = lax.broadcasted_iota(jnp.int32, (8, sensors), 0)
    sums_py[0] = jnp.where(line == 0, partial, jnp.where(line == 1, own, 0.0))

    def all_sum(sums, count, me, axis, sent, got):
        copies = []
        for step in range(1, count):
            move = pltpu.make_async_remote_copy(
                src_ref=sums.at[0], dst_ref=sums.at[step], send_sem=sent.at[step], recv_sem=got.at[step],
                device_id={axis: lax.rem(me + step, count)}, device_id_type=MESH,
            )
            move.start()
            copies.append(move)
        total = sums[0]
        for step, move in enumerate(copies):
            move.wait()
            total = total + sums[step + 1]
        return total

    sums_px[0] = all_sum(sums_py, n_py, py, "py", py_send, py_recv)
    total = all_sum(sums_px, n_px, px, "px", px_send, px_recv)
    weighted = total[0:1] * total[1:2]
    returned = jnp.dot(split_rows(weighted), key_hot[...], preferred_element_type=jnp.float32)
    returned = jnp.sum(returned, axis=0, keepdims=True)

    for kind in range(kinds):
        columns = slice(kind * probes, (kind + 1) * probes)
        value = weights[kind : kind + 1, :] * returned
        high = value.astype(jnp.bfloat16)
        low = (value - high.astype(jnp.float32)).astype(jnp.bfloat16)
        row_val[0:nodes_dev, columns] = row_hot[:, columns] * high
        row_val[nodes_dev:, columns] = row_hot[:, columns] * low

    for block in range(depth // tall):
        span = slice(block * tall, (block + 1) * tall)
        both = lax.dot_general(row_val[...], z_hot[span, :], contract_lanes, preferred_element_type=jnp.float32)
        both = (both[:nodes_dev] + both[nodes_dev:]).reshape(rows, cols, tall)
        remain[:, :, span] = both
        search[0, :, :, span] = both / centre
    for strip in order:
        send_outer(ADJ, search.at[0])(strip)
    send_inner(ADJ, search.at[0])

    solve(ADJ)

    end = ADJ + SWEEPS - 1

    def sum_halo(halo, at):
        halo[(end,) + at] = (halo[(ADJ,) + at] + halo[(ADJ + 1,) + at]) + (halo[(ADJ + 2,) + at] + halo[(end,) + at])

    def sense_work(x, strip, below, above):
        y = strip * STRIP
        b, b_near = around(back, below[0], above[0], BACK, x, strip)
        a, a_near = around(remain, below[1], above[1], end, x, strip)
        terms = [(b - bn) * (a - an) for bn, an in zip(b_near, a_near)]
        total = terms[0] + terms[1] + terms[2] + terms[3]
        total = total + jnp.where(first_lane, 0.0, terms[4]) + jnp.where(last_lane, 0.0, terms[5])
        out[x, y : y + STRIP, :] = total

    def sum_strip(strip):
        for side, edge in ((0, 0), (1, strips - 1)):
            sum_halo(halo_x, (side, slice(strip * STRIP, (strip + 1) * STRIP)))
            if strip == edge:
                sum_halo(halo_y, (1, side))

    newest = search.at[SWEEPS - 1]
    for side in range(2):
        take_y(end, side, 0)
        sum_halo(halo_y, (0, side))
    inner_planes(sense_work, (), (back, remain))
    for strip in order:
        take_x(end, strip, newest)
        for side, edge in ((0, 0), (1, strips - 1)):
            if strip == edge:
                take_y(end, side, 1)
        sum_strip(strip)
        sense_work(0, strip, [halo_x.at[BACK, 0], halo_x.at[end, 0]], [back.at[1], remain.at[1]])
        sense_work(last, strip, [back.at[last - 1], remain.at[last - 1]], [halo_x.at[BACK, 1], halo_x.at[end, 1]])
    sent(end, (0, 1), newest)


def body(back, pert, permit, nodes, weights, owner, sensor, sensor_weight):
    n_px, n_py = lax.axis_size("px"), lax.axis_size("py")
    rows, cols, depth = back.shape
    kinds, probes = nodes.shape
    sensors = sensor_weight.shape[0] * n_px * n_py
    nodes_dev = rows * cols
    f32, bf16 = jnp.float32, jnp.bfloat16
    vmem = pl.BlockSpec(memory_space=pltpu.VMEM)
    smem = pl.BlockSpec(memory_space=pltpu.SMEM)
    block = pltpu.VMEM((rows, cols, depth), f32)
    dma = pltpu.SemaphoreType.DMA
    doubled = pl.pallas_call(
        functools.partial(kernel, n_px, n_py),
        out_shape=jax.ShapeDtypeStruct((rows, cols, depth), f32),
        in_specs=[vmem] * 7 + [smem],
        out_specs=vmem,
        scratch_shapes=[
            pltpu.VMEM((SWEEPS, rows, cols, depth), f32),
            block,
            pltpu.VMEM((rows + 1, cols, depth), f32),
            block, block, block, block, block,
            pltpu.VMEM((EXCHANGES, 2, cols, depth), f32),
            pltpu.VMEM((EXCHANGES, 2, 2, rows, depth), f32),
            pltpu.VMEM((EXCHANGES, 2, 2, rows, depth), f32),
            pltpu.VMEM((depth, 2 * nodes_dev), bf16),
            pltpu.VMEM((nodes_dev, kinds * probes), bf16),
            pltpu.VMEM((2 * nodes_dev, kinds * probes), bf16),
            pltpu.VMEM((depth, kinds * probes), bf16),
            pltpu.VMEM((sensors, probes), bf16),
            pltpu.VMEM((1, probes), f32),
            pltpu.VMEM((n_py, 8, sensors), f32),
            pltpu.VMEM((n_px, 8, sensors), f32),
            dma((EXCHANGES, 2, cols // STRIP)), dma((EXCHANGES, 2, cols // STRIP)),
            dma((EXCHANGES, 2, 2)), dma((EXCHANGES, 2, 2)),
            dma((n_py,)), dma((n_py,)), dma((n_px,)), dma((n_px,)),
        ],
        compiler_params=pltpu.CompilerParams(
            collective_id=0, has_side_effects=True, vmem_limit_bytes=46 * 1024 * 1024
        ),
        cost_estimate=pl.CostEstimate(flops=10_000_000_000, bytes_accessed=4_500_000, transcendentals=0),
    )(
        back, pert, permit, nodes, weights, owner.reshape(1, probes), sensor.reshape(1, probes), sensor_weight
    )
    return -0.5 * doubled


def solution(mesh):
    placed = (
        P("px", "py", None),
        P("px", "py", None),
        P("px", "py", None),
        P(None, ("px", "py")),
        P(None, ("px", "py")),
        P(("px", "py"), None),
        P(("px", "py")),
        P(("px", "py")),
    )
    return jax.shard_map(
        body, mesh=mesh, in_specs=placed, out_specs=P("px", "py", None), check_vma=False
    )
```
